256 devices in a mesh: gy: 32 (over x, z_hi, core), gz: 8 (over z_lo, y).
Axes of the slice: x: 4, y: 4, z: 8 (z_hi: 4, z_lo: 2; z = z_hi * 2 + z_lo), core: 2. Of those that a mesh axis runs over, the one named last changes fastest.
Arguments:
- coeffs: bfloat16 [3, 512, 512, 512], P(None, 'gy', 'gz'), may hold values from -6 to 6
Outputs:
- current: float32 [3, 512, 512, 512], P(None, 'gy', 'gz')
- picture: float32 [4, 512, 512], P(None, 'gz', 'gy')
The draws below stay inside these ranges and needn't reach their ends.
All inputs are finite; a program needn't handle non-finite values.
Results may differ from the reference program's by a relative error of at most 0.0051.
The reference program's roundings to bfloat16 on the way (of `basis_table`, `along_z` and `along_y`) count: a program that leaves them out, or rounds other values in their place, can miss the bound.
Values may be sent and summed in bfloat16 or wider, within the bound.
A program may use at most 128 MiB of HBM per device.

```python
import math
import jax
import jax.numpy as jnp
from jax import lax

N = 512


def level_of(key, shape, cuts, smallest, high):
    loudness, own = 1.0, jax.random.fold_in(key, 6)
    for dim, blocks in cuts:
        steps = jnp.exp(jax.random.uniform(jax.random.fold_in(own, dim), (blocks,), jnp.float32, smallest / len(cuts), high / len(cuts)))
        loudness = loudness * jnp.repeat(steps, shape[dim] // blocks).reshape([-1 if axis == dim else 1 for axis in range(len(shape))])
    return loudness


def gaussian(stream_key, extent, width, most, cuts=(), held_as=jnp.bfloat16):
    array = width * jax.random.normal(stream_key, extent, jnp.float32)
    if cuts:
        array = array * level_of(stream_key, extent, cuts, -0.22, 0.18)
    return jnp.clip(array, -most, most).astype(held_as)


def setup_inputs(seed: int = 0) -> dict:
    key_of = jax.random.split(jax.random.key(seed), 2)
    coeffs = gaussian(key_of[0], (3, N, N, N), 1.0, 6.0, ((1, 32), (2, 8)))
    return dict(coeffs=coeffs)


def make_basis(length):
    mode_index = jnp.arange(length, dtype=jnp.int32)[:, None]
    cell_index = jnp.arange(length, dtype=jnp.int32)[None, :]
    half_size = length // 2
    frequency = jnp.where(mode_index <= half_size, mode_index, mode_index - half_size)
    phase_angle = (frequency * cell_index % length).astype(jnp.float32) * (2.0 * math.pi / length)
    values = jnp.where(mode_index <= half_size, jnp.cos(phase_angle), jnp.sin(phase_angle)) * math.sqrt(2.0 / length)
    return values.astype(jnp.bfloat16)

def colormap(density):
    red_level = jnp.clip((density - 2.0) / 3.0, 0.0, 1.0)
    green_level = jnp.clip(1.0 - jnp.abs(density - 3.0) / 2.0, 0.0, 1.0)
    blue_level = jnp.clip(1.0 - density / 2.0, 0.0, 1.0)
    return 4.0 * jnp.stack([red_level, green_level, blue_level], axis=0)

def reference(coeffs):
    basis_table = make_basis(N)
    fields = []
    density = jnp.zeros((N, N, N), jnp.float32)
    for component in range(3):
        flat_modes = coeffs[component].reshape(N * N, N)
        along_z = jnp.dot(flat_modes, basis_table, preferred_element_type=jnp.float32).astype(jnp.bfloat16).reshape(N, N, N)
        swapped = along_z.transpose(0, 2, 1).reshape(N * N, N)
        along_y = jnp.dot(swapped, basis_table, preferred_element_type=jnp.float32).astype(jnp.bfloat16).reshape(N, N, N)
        final_order = along_y.transpose(2, 1, 0).reshape(N * N, N)
        physical = jnp.dot(final_order, basis_table, preferred_element_type=jnp.float32).reshape(N, N, N)
        fields.append(physical)
        density = density + physical * physical
    absorb = 0.6 / N

    def march_layer(state_pair, layer_row):
        depth_sum, color_sum = state_pair
        optical = absorb * layer_row
        weight = jnp.exp(-depth_sum) * (1.0 - jnp.exp(-optical))
        color_sum = color_sum + weight[None] * colormap(layer_row)
        return ((depth_sum + optical, color_sum), None)
    initial = (jnp.zeros((N, N), jnp.float32), jnp.zeros((3, N, N), jnp.float32))
    (depth_sum, color_sum), ignored = lax.scan(march_layer, initial, density)
    coverage = 1.0 - jnp.exp(-depth_sum)
    picture = jnp.concatenate([color_sum, coverage[None]], axis=0)
    return (jnp.stack(fields, axis=0), picture)
```

```python
import functools
import math

import jax
import jax.numpy as jnp
import ml_dtypes
import numpy as np
from jax import lax
from jax.experimental import pallas as pl
from jax.experimental.pallas import tpu as pltpu
from jax.sharding import PartitionSpec as P

N = 512
J = 4
ZC = 16
MESH = pl.DeviceIdType.MESH
BF, F32 = jnp.bfloat16, jnp.float32


def make_basis(length):
    mode_index = np.arange(length, dtype=np.int32)[:, None]
    cell_index = np.arange(length, dtype=np.int32)[None, :]
    half_size = length // 2
    frequency = np.where(mode_index <= half_size, mode_index, mode_index - half_size)
    phase_angle = (frequency * cell_index % length).astype(np.float32) * np.float32(2.0 * math.pi / length)
    values = np.where(mode_index <= half_size, np.cos(phase_angle), np.sin(phase_angle)) * np.float32(
        math.sqrt(2.0 / length)
    )
    return values.astype(ml_dtypes.bfloat16)


def tables():
    basis = make_basis(N)
    order_z = np.arange(N).reshape(8, J, ZC).transpose(1, 0, 2).reshape(-1)
    table_z = np.ascontiguousarray(basis.T[order_z])
    table_y = np.zeros((2, N, 8, 2, 64), ml_dtypes.bfloat16)
    for parity in range(2):
        table_y[parity, :, :, parity, :] = basis.T.reshape(N, 8, 64)
    table_y = table_y.reshape(2 * N, 2 * N)
    group, pair, tile = np.meshgrid(np.arange(4), np.arange(8), np.arange(16), indexing="ij")
    slot = group * 16 + tile
    order_x = ((slot // 2) * 16 + pair * 2 + slot % 2).reshape(-1)
    table_x = np.ascontiguousarray(basis[order_x])
    return table_z, table_y, table_x


def kernel(
    coef_hbm, tz_hbm, ty_hbm, tx_hbm, current_hbm, bricks_ref,
    coef, tz, ty, tx, sent1, got1, sent2, got2, rows_x, field, tint, pic_out, pic_in,
    load_sem, send1, recv1, send2, recv2, send3, recv3, store_sem,
):
    gy, gz = lax.axis_index("gy"), lax.axis_index("gz")

    def gy_at(step):
        gx = lax.rem(gy // 8 + step // 8, 4)
        gh = lax.rem(lax.rem(gy // 2, 4) + lax.rem(step // 2, 4), 4)
        gc = lax.rem(gy + step, 2)
        return gx * 8 + gh * 2 + gc

    def gz_at(step):
        return lax.rem(gz // 4 + step // 4, 2) * 4 + lax.rem(gz + step, 4)

    barrier = pltpu.get_barrier_semaphore()

    def greet_z(step, carry):
        pl.semaphore_signal(barrier, inc=1, device_id=(gy, gz_at(step)), device_id_type=MESH)
        return carry

    def greet_y(step, carry):
        pl.semaphore_signal(barrier, inc=1, device_id=(gy_at(step), gz), device_id_type=MESH)
        return carry

    loads = [
        pltpu.make_async_copy(tz_hbm, tz, load_sem.at[0]),
        pltpu.make_async_copy(coef_hbm, coef, load_sem.at[1]),
        pltpu.make_async_copy(ty_hbm, ty, load_sem.at[2]),
        pltpu.make_async_copy(tx_hbm, tx, load_sem.at[3]),
    ]
    for load in loads:
        load.start()
    lax.fori_loop(1, 8, greet_z, 0)
    lax.fori_loop(1, 32, greet_y, 0)
    loads[0].wait()
    loads[1].wait()

    def transform_z(chunk):
        def one(p, carry):
            out = lax.dot_general(
                tz[pl.ds(chunk * 128, 128), :], coef[p], (((1,), (1,)), ((), ())), preferred_element_type=F32
            ).astype(BF)
            for q in range(8):
                sent1[chunk, q, p] = out[q * ZC : (q + 1) * ZC]
            return carry

        lax.fori_loop(0, 24, one, 0, unroll=4)

    def send_z(chunk):
        pltpu.make_async_copy(sent1.at[chunk, gz], got1.at[chunk, gz], recv1.at[chunk]).start()

        def one(step, carry):
            to = gz_at(step)
            pltpu.make_async_remote_copy(
                src_ref=sent1.at[chunk, to], dst_ref=got1.at[chunk, gz],
                send_sem=send1.at[chunk], recv_sem=recv1.at[chunk],
                device_id=(gy, to), device_id_type=MESH,
            ).start()
            return carry

        lax.fori_loop(1, 8, one, 0)

    transform_z(0)
    pl.semaphore_wait(barrier, 38)

    def stage_z(chunk, carry):
        send_z(chunk)

        @pl.when(chunk < J - 1)
        def _():
            transform_z(chunk + 1)

        return carry

    lax.fori_loop(0, J, stage_z, 0)
    loads[2].wait()
    loads[3].wait()

    def stage_y(chunk, carry):
        pltpu.make_async_copy(got1.at[chunk], got1.at[chunk], recv1.at[chunk]).wait()

        def one(c, inner):
            rows = jnp.concatenate(
                [got1[chunk, s, pl.ds(c * 8, 8)].reshape(128, 128) for s in range(8)], axis=1
            )
            for half in range(2):
                out = lax.dot_general(
                    ty[half * N : (half + 1) * N, :], rows, (((1,), (1,)), ((), ())), preferred_element_type=F32
                ).astype(BF)
                for g in range(32):
                    sent2[chunk, g, c, half] = out[g * 16 : (g + 1) * 16]
            return inner

        lax.fori_loop(0, 3, one, 0)
        pltpu.make_async_copy(sent2.at[chunk, gy], got2.at[chunk, gy], recv2.at[chunk]).start()

        def push(step, inner):
            to = gy_at(step)
            pltpu.make_async_remote_copy(
                src_ref=sent2.at[chunk, to], dst_ref=got2.at[chunk, gy],
                send_sem=send2.at[chunk], recv_sem=recv2.at[chunk],
                device_id=(to, gz), device_id_type=MESH,
            ).start()
            return inner

        lax.fori_loop(1, 32, push, 0)
        return carry

    lax.fori_loop(0, J, stage_y, 0)

    lane = lax.broadcasted_iota(jnp.int32, (16, 128), 1)

    def stage_x(chunk, carry):
        pltpu.make_async_copy(got2.at[chunk], got2.at[chunk], recv2.at[chunk]).wait()

        def component(c, inner):
            for group in range(4):
                tiles = [got2[chunk, group * 8 + t // 2, c, t % 2].astype(F32) for t in range(16)]
                for bit in (1, 2, 4, 8):
                    low = (lane & bit) == 0
                    for t in range(16):
                        if t & bit == 0:
                            u, v = tiles[t], tiles[t + bit]
                            tiles[t] = jnp.where(low, u, pltpu.roll(v, bit, 1))
                            tiles[t + bit] = jnp.where(low, pltpu.roll(u, 128 - bit, 1), v)
                for t in range(16):
                    rows_x[pl.ds(t * 16, 16), pl.ds(group * 128, 128)] = tiles[t].astype(BF)
            out = jnp.dot(rows_x[...], tx[...], preferred_element_type=F32)
            for col in range(4):
                for t in range(16):
                    field[chunk, c, col, pl.ds(t, 16, stride=ZC), :] = out[
                        t * 16 : (t + 1) * 16, col * 128 : (col + 1) * 128
                    ]
                pltpu.make_async_copy(
                    field.at[chunk, c, col].reshape(16, ZC, 128),
                    current_hbm.at[c, :, pl.ds(chunk * ZC, ZC), pl.ds(col * 128, 128)],
                    store_sem.at[chunk, c],
                ).start()
            return inner

        lax.fori_loop(0, 3, component, 0)
        absorb = 0.6 / N
        for col in range(4):
            cols = pl.ds(col * 128, 128)
            passed = jnp.ones((ZC, 128), F32)
            depth = jnp.zeros((ZC, 128), F32)
            colors = [jnp.zeros((ZC, 128), F32)] * 3
            for y in range(16):
                parts = [field[chunk, c, col, pl.ds(y * ZC, ZC), :] for c in range(3)]
                density = parts[0] * parts[0] + parts[1] * parts[1] + parts[2] * parts[2]
                optical = absorb * density
                left = jnp.exp(-optical)
                weight = 4.0 * (passed * (1.0 - left))
                passed = passed * left
                depth = depth + optical
                levels = (
                    jnp.clip((density - 2.0) * (1.0 / 3.0), 0.0, 1.0),
                    jnp.clip(1.0 - jnp.abs(density - 3.0) * 0.5, 0.0, 1.0),
                    jnp.clip(1.0 - density * 0.5, 0.0, 1.0),
                )
                colors = [color + weight * level for color, level in zip(colors, levels)]
            part = lax.rem(chunk, 2)
            for k, value in enumerate(colors + [depth]):
                tint[pl.ds(part * 64 + k * ZC, ZC), cols] = value

        @pl.when(lax.rem(chunk, 2) == 1)
        def _():
            pair = chunk // 2
            for col in range(4):
                turned = jnp.transpose(tint[:, col * 128 : (col + 1) * 128]).astype(BF)
                for g in range(8):
                    pic_out[pair, col * 8 + g] = turned[g * 16 : (g + 1) * 16]
            pltpu.make_async_copy(pic_out.at[pair, gy], pic_in.at[pair, gy], recv3.at[pair]).start()

            def push(step, inner):
                to = gy_at(step)
                pltpu.make_async_remote_copy(
                    src_ref=pic_out.at[pair, to], dst_ref=pic_in.at[pair, gy],
                    send_sem=send3.at[pair], recv_sem=recv3.at[pair],
                    device_id=(to, gz), device_id_type=MESH,
                ).start()
                return inner

            lax.fori_loop(1, 32, push, 0)

        return carry

    lax.fori_loop(0, J, stage_x, 0)

    channel = (lane // ZC) % 4
    is_depth = channel == 3

    def combine(pair, carry):
        pltpu.make_async_copy(pic_in.at[pair], pic_in.at[pair], recv3.at[pair]).wait()
        before = jnp.zeros((16, 128), F32)
        total = jnp.zeros((16, 128), F32)
        for s in range(32):
            brick = pic_in[pair, s].astype(F32)
            depth = jnp.where(is_depth, brick, 0.0)
            depth = depth + pltpu.roll(depth, 128 - 16, 1)
            depth = depth + pltpu.roll(depth, 128 - 32, 1)
            total = total + jnp.exp(-before) * brick
            before = before + depth
        bricks_ref[pair] = jnp.where(is_depth, 1.0 - jnp.exp(-before), total)
        return carry

    lax.fori_loop(0, 2, combine, 0)

    for chunk in range(J):
        first = sent1.at[chunk, pl.ds(0, 7)]
        pltpu.make_async_copy(first, first, send1.at[chunk]).wait()
        second = sent2.at[chunk, pl.ds(0, 31)]
        pltpu.make_async_copy(second, second, send2.at[chunk]).wait()
        for c in range(3):
            pltpu.make_async_copy(field.at[chunk, c], field.at[chunk, c], store_sem.at[chunk, c]).wait()
    for pair in range(2):
        third = pic_out.at[pair, pl.ds(0, 31)]
        pltpu.make_async_copy(third, third, send3.at[pair]).wait()


def shards(coeffs):
    table_z, table_y, table_x = (jnp.asarray(table) for table in tables())
    any_space = pl.BlockSpec(memory_space=pl.ANY)
    current, bricks = pl.pallas_call(
        kernel,
        out_shape=(
            jax.ShapeDtypeStruct((3, 16, 64, N), F32),
            jax.ShapeDtypeStruct((2, 16, 128), F32),
        ),
        in_specs=[any_space] * 4,
        out_specs=(any_space, pl.BlockSpec(memory_space=pltpu.VMEM)),
        scratch_shapes=[
            pltpu.VMEM((24, 128, N), BF),
            pltpu.VMEM((N, N), BF),
            pltpu.VMEM((2 * N, 2 * N), BF),
            pltpu.VMEM((N, N), BF),
            pltpu.VMEM((J, 8, 24, ZC, 128), BF),
            pltpu.VMEM((J, 8, 24, ZC, 128), BF),
            pltpu.VMEM((J, 32, 3, 2, 16, 128), BF),
            pltpu.VMEM((J, 32, 3, 2, 16, 128), BF),
            pltpu.VMEM((256, N), BF),
            pltpu.VMEM((J, 3, 4, 16 * ZC, 128), F32),
            pltpu.VMEM((128, N), F32),
            pltpu.VMEM((2, 32, 16, 128), BF),
            pltpu.VMEM((2, 32, 16, 128), BF),
            pltpu.SemaphoreType.DMA((4,)),
            pltpu.SemaphoreType.DMA((J,)),
            pltpu.SemaphoreType.DMA((J,)),
            pltpu.SemaphoreType.DMA((J,)),
            pltpu.SemaphoreType.DMA((J,)),
            pltpu.SemaphoreType.DMA((2,)),
            pltpu.SemaphoreType.DMA((2,)),
            pltpu.SemaphoreType.DMA((J, 3)),
        ],
        compiler_params=pltpu.CompilerParams(
            collective_id=0, has_side_effects=True, vmem_limit_bytes=48 * 1024 * 1024
        ),
        name="render",
    )(coeffs.reshape(24, 128, N), table_z, table_y, table_x)
    picture = bricks.reshape(2, 16, 2, 4, ZC).transpose(3, 0, 2, 4, 1).reshape(4, 64, 16)
    return (current, picture)


def solution(mesh):
    return jax.shard_map(
        shards,
        mesh=mesh,
        in_specs=(P(None, "gy", "gz", None),),
        out_specs=(P(None, "gy", "gz", None), P(None, "gz", "gy")),
        check_vma=False,
    )
```

```python
import functools
import math

import jax
import jax.numpy as jnp
import ml_dtypes
import numpy as np
from jax import lax
from jax.experimental import pallas as pl
from jax.experimental.pallas import tpu as pltpu
from jax.sharding import PartitionSpec as P

N = 512
J = 4
ZC = 16
MESH = pl.DeviceIdType.MESH
BF, F32 = jnp.bfloat16, jnp.float32


def make_basis(length):
    mode_index = np.arange(length, dtype=np.int32)[:, None]
    cell_index = np.arange(length, dtype=np.int32)[None, :]
    half_size = length // 2
    frequency = np.where(mode_index <= half_size, mode_index, mode_index - half_size)
    phase_angle = (frequency * cell_index % length).astype(np.float32) * np.float32(2.0 * math.pi / length)
    values = np.where(mode_index <= half_size, np.cos(phase_angle), np.sin(phase_angle)) * np.float32(
        math.sqrt(2.0 / length)
    )
    return values.astype(ml_dtypes.bfloat16)


SLOTS = 136
PAIRS = ((0, 3), (1, 2))


def cells_of(half):
    blocks = [x * 8 + hi * 2 + core for x in range(4) for hi in PAIRS[half] for core in range(2)]
    return np.array([block * 16 + i for block in blocks for i in range(16)])


def slots_of(z_lo, half):
    cells = cells_of(half)
    folded = sorted(set(np.minimum(cells, N - cells).tolist()))
    if z_lo == 1:
        folded = [cell for cell in folded if cell not in (0, N // 2)]
    return folded


def tables():
    basis = make_basis(N).astype(np.float32)
    order_z = np.arange(N).reshape(2, 4, J, ZC).transpose(2, 1, 0, 3).reshape(-1)
    table_z = np.ascontiguousarray(basis.T[order_z])
    keep = np.zeros((4, 2, 256, 4, 2, 64), np.float32)
    give = np.zeros((4, 2, SLOTS, 4, 2, 64), np.float32)
    take = np.zeros((4, 2, 256, 2, SLOTS), np.float32)
    for z_lo in range(2):
        modes = slice(z_lo * 256, z_lo * 256 + 256)
        for half in range(2):
            kind = z_lo * 2 + half
            cells = cells_of(half)
            own = basis[modes, :][:, cells].T.reshape(256, 4, 64)
            slots = slots_of(z_lo, 1 - half)
            sums = np.zeros((SLOTS, 256), np.float32)
            sums[: len(slots)] = basis[modes, :][:, slots].T
            if z_lo == 1:
                sums[:, 0] = 0.0
                sums[len(slots), 0] = basis[256, 0]
            unfold = np.zeros((256, SLOTS), np.float32)
            theirs = slots_of(1 - z_lo, half)
            for row, cell in enumerate(cells):
                folded = min(cell, N - cell)
                if folded in theirs:
                    unfold[row, theirs.index(folded)] = 1.0 if z_lo == 1 or cell < N // 2 else -1.0
                if z_lo == 0:
                    unfold[row, len(theirs)] = 1.0 - 2.0 * (cell % 2)
            for parity in range(2):
                keep[kind, parity, :, :, parity] = own
                give[kind, parity, :, :, parity] = sums.reshape(SLOTS, 4, 64)
                take[kind, parity, :, parity] = unfold
    group, pair, tile = np.meshgrid(np.arange(4), np.arange(8), np.arange(16), indexing="ij")
    slot = group * 16 + tile
    order_x = ((slot // 2) * 16 + pair * 2 + slot % 2).reshape(-1)
    table_x = np.ascontiguousarray(basis[order_x])
    return (
        table_z,
        np.concatenate([keep.reshape(4, 512, 512), give.reshape(4, 2 * SLOTS, 512)], axis=1),
        take.reshape(4, 512, 2 * SLOTS),
        table_x,
    )


def kernel(
    coef_hbm, tz_hbm, ty_hbm, take_hbm, tx_hbm, current_hbm, bricks_ref,
    raw_z, raw_y, raw_take, raw_x,
    coef, tz, ty, take, tx, sent1, got1, half_out, half_in, sent2, got2, rows_x, field, tint, pic_out, pic_in,
    load_sem, send1, recv1, sendh, recvh, send2, recv2, send3, recv3, store_sem,
):
    gy, gz = lax.axis_index("gy"), lax.axis_index("gz")
    at_x, at_hi, at_core = gy // 8, lax.rem(gy // 2, 4), lax.rem(gy, 2)
    at_lo, at_y = gz // 4, lax.rem(gz, 4)
    half = lax.rem(at_lo + at_hi // 2, 2)
    kind = at_lo * 2 + half
    in_half = half == lax.rem((at_hi + 1) // 2, 2)

    def gy_at(step):
        gx = lax.rem(at_x + step // 8, 4)
        gh = lax.rem(at_hi + lax.rem(step // 2, 4), 4)
        gc = lax.rem(at_core + step, 2)
        return gx * 8 + gh * 2 + gc

    def y_at(step):
        return at_lo * 4 + lax.rem(at_y + step, 4)

    twin = (1 - at_lo) * 4 + at_y

    barrier = pltpu.get_barrier_semaphore()

    def greet(step, carry):
        to = gy_at(step)
        pl.semaphore_signal(barrier, inc=1, device_id=(to, gz), device_id_type=MESH)
        pl.semaphore_signal(barrier, inc=1, device_id=(to, twin), device_id_type=MESH)
        return carry

    loads = [
        pltpu.make_async_copy(tz_hbm, raw_z, load_sem.at[0]),
        pltpu.make_async_copy(coef_hbm, coef, load_sem.at[1]),
        pltpu.make_async_copy(ty_hbm.at[kind], raw_y, load_sem.at[2]),
        pltpu.make_async_copy(take_hbm.at[kind], raw_take, load_sem.at[3]),
        pltpu.make_async_copy(tx_hbm, raw_x, load_sem.at[4]),
    ]
    for load in loads:
        load.start()
    for step in range(1, 4):
        pl.semaphore_signal(barrier, inc=1, device_id=(gy, y_at(step)), device_id_type=MESH)
    pl.semaphore_signal(barrier, inc=1, device_id=(gy, twin), device_id_type=MESH)
    lax.fori_loop(1, 32, greet, 0)
    loads[0].wait()
    tz[...] = raw_z[...].astype(BF)
    loads[1].wait()

    def transform_z(unit):
        chunk, c = unit // 3, lax.rem(unit, 3)

        def one(p, carry):
            out = lax.dot_general(
                tz[pl.ds(pl.multiple_of(chunk * 128, 128), 128), :], coef[c * 8 + p], (((1,), (1,)), ((), ())),
                preferred_element_type=F32,
            ).astype(BF)
            for y in range(4):
                for lo in range(2):
                    row = (y * 2 + lo) * ZC
                    sent1[chunk, c, y, lo, p] = out[row : row + ZC]
            return carry

        lax.fori_loop(0, 8, one, 0, unroll=4)

    def send_z(unit):
        chunk, c = unit // 3, lax.rem(unit, 3)
        pltpu.make_async_copy(sent1.at[chunk, c, at_y], got1.at[chunk, c, at_y], recv1.at[chunk, c]).start()
        for step in range(1, 4):
            to = lax.rem(at_y + step, 4)
            pltpu.make_async_remote_copy(
                src_ref=sent1.at[chunk, c, to], dst_ref=got1.at[chunk, c, at_y],
                send_sem=send1.at[chunk, c], recv_sem=recv1.at[chunk, c],
                device_id=(gy, at_lo * 4 + to), device_id_type=MESH,
            ).start()

    transform_z(0)
    pl.semaphore_wait(barrier, 66)

    def stage_z(unit, carry):
        send_z(unit)

        @pl.when(unit < 3 * J - 1)
        def _():
            transform_z(unit + 1)

        return carry

    lax.fori_loop(0, 3 * J, stage_z, 0)
    loads[2].wait()
    loads[3].wait()
    loads[4].wait()
    ty[...] = raw_y[...].astype(BF)
    take[...] = raw_take[...].astype(BF)
    tx[...] = raw_x[...].astype(BF)

    def rows_of(chunk, c):
        return jnp.concatenate([got1[chunk, c, s].reshape(256, 128) for s in range(4)], axis=1)

    def half_copy(chunk, c):
        return pltpu.make_async_remote_copy(
            src_ref=half_out.at[chunk, c], dst_ref=half_in.at[chunk, c],
            send_sem=sendh.at[chunk, c], recv_sem=recvh.at[chunk, c],
            device_id=(gy, twin), device_id_type=MESH,
        )

    def push_y(chunk):
        def push(step, carry):
            to_x = lax.rem(at_x + step // 8, 4)
            place = lax.rem(step // 4 + at_hi, 2)
            to_hi = jnp.where(half == 0, 3 * place, 1 + place)
            to_lo = lax.rem(step // 2 + at_lo, 2)
            to_core = lax.rem(step + at_core, 2)
            slot = (to_x * 4 + place * 2 + to_core) * 2 + to_lo
            to = to_x * 8 + to_hi * 2 + to_core
            same = jnp.logical_and(to == gy, to_lo == at_lo)

            @pl.when(same)
            def _():
                pltpu.make_async_copy(sent2.at[chunk, slot], got2.at[chunk, gy], recv2.at[chunk]).start()

            @pl.when(jnp.logical_not(same))
            def _():
                pltpu.make_async_remote_copy(
                    src_ref=sent2.at[chunk, slot], dst_ref=got2.at[chunk, gy],
                    send_sem=send2.at[chunk], recv_sem=recv2.at[chunk],
                    device_id=(to, to_lo * 4 + at_y), device_id_type=MESH,
                ).start()

            return carry

        lax.fori_loop(0, 32, push, 0)

    def stage_y(unit, carry):
        @pl.when(unit < 3 * J)
        def _():
            chunk, c = unit // 3, lax.rem(unit, 3)
            pltpu.make_async_copy(got1.at[chunk, c], got1.at[chunk, c], recv1.at[chunk, c]).wait()
            half_out[chunk, c] = lax.dot_general(
                ty[512:, :], rows_of(chunk, c), (((1,), (1,)), ((), ())), preferred_element_type=F32
            ).astype(BF)
            half_copy(chunk, c).start()

        @pl.when(unit >= 1)
        def _():
            chunk, c = (unit - 1) // 3, lax.rem(unit - 1, 3)
            half_copy(chunk, c).wait_recv()
            rows = rows_of(chunk, c)
            theirs = half_in[chunk, c]
            for parity in range(2):
                out = lax.dot_general(
                    ty[parity * 256 : parity * 256 + 256, :], rows, (((1,), (1,)), ((), ())), preferred_element_type=F32
                )
                out = out + jnp.dot(
                    take[parity * 256 : parity * 256 + 256, :], theirs, preferred_element_type=F32
                )
                out = out.astype(BF)
                for d in range(16):
                    for lo in range(2):
                        sent2[chunk, d * 2 + lo, c, parity] = out[d * 16 : d * 16 + 16, lo * 128 : lo * 128 + 128]

            @pl.when(c == 2)
            def _():
                push_y(chunk)

        return carry

    lax.fori_loop(0, 3 * J + 1, stage_y, 0)

    lane = lax.broadcasted_iota(jnp.int32, (16, 128), 1)

    def stage_x(chunk, carry):
        pltpu.make_async_copy(got2.at[chunk], got2.at[chunk], recv2.at[chunk]).wait()

        def component(c, inner):
            for group in range(4):
                tiles = [got2[chunk, group * 8 + t // 2, c, t % 2].astype(F32) for t in range(16)]
                for bit in (1, 2, 4, 8):
                    low = (lane & bit) == 0
                    for t in range(16):
                        if t & bit == 0:
                            u, v = tiles[t], tiles[t + bit]
                            tiles[t] = jnp.where(low, u, pltpu.roll(v, bit, 1))
                            tiles[t + bit] = jnp.where(low, pltpu.roll(u, 128 - bit, 1), v)
                for t in range(16):
                    rows_x[pl.ds(t * 16, 16), pl.ds(group * 128, 128)] = tiles[t].astype(BF)
            out = jnp.dot(rows_x[...], tx[...], preferred_element_type=F32)
            for col in range(4):
                for t in range(16):
                    field[chunk, c, col, pl.ds(t, 16, stride=ZC), :] = out[
                        t * 16 : (t + 1) * 16, col * 128 : (col + 1) * 128
                    ]
                pltpu.make_async_copy(
                    field.at[chunk, c, col].reshape(16, ZC, 128),
                    current_hbm.at[c, :, pl.ds(chunk * ZC, ZC), pl.ds(col * 128, 128)],
                    store_sem.at[chunk, c],
                ).start()
            return inner

        lax.fori_loop(0, 3, component, 0)
        absorb = 0.6 / N
        for col in range(4):
            cols = pl.ds(col * 128, 128)
            passed = jnp.ones((ZC, 128), F32)
            depth = jnp.zeros((ZC, 128), F32)
            colors = [jnp.zeros((ZC, 128), F32)] * 3
            for y in range(16):
                parts = [field[chunk, c, col, pl.ds(y * ZC, ZC), :] for c in range(3)]
                density = parts[0] * parts[0] + parts[1] * parts[1] + parts[2] * parts[2]
                optical = absorb * density
                left = jnp.exp(-optical)
                weight = 4.0 * (passed * (1.0 - left))
                passed = passed * left
                depth = depth + optical
                levels = (
                    jnp.clip((density - 2.0) * (1.0 / 3.0), 0.0, 1.0),
                    jnp.clip(1.0 - jnp.abs(density - 3.0) * 0.5, 0.0, 1.0),
                    jnp.clip(1.0 - density * 0.5, 0.0, 1.0),
                )
                colors = [color + weight * level for color, level in zip(colors, levels)]
            part = lax.rem(chunk, 2)
            for k, value in enumerate(colors + [depth]):
                tint[pl.ds(part * 64 + k * ZC, ZC), cols] = value

        @pl.when(lax.rem(chunk, 2) == 1)
        def _():
            pair = chunk // 2
            for col in range(4):
                turned = jnp.transpose(tint[:, col * 128 : (col + 1) * 128]).astype(BF)
                for g in range(8):
                    pic_out[pair, col * 8 + g] = turned[g * 16 : (g + 1) * 16]
            pltpu.make_async_copy(pic_out.at[pair, gy], pic_in.at[pair, gy], recv3.at[pair]).start()

            def push(step, inner):
                to = gy_at(step)
                pltpu.make_async_remote_copy(
                    src_ref=pic_out.at[pair, to], dst_ref=pic_in.at[pair, gy],
                    send_sem=send3.at[pair], recv_sem=recv3.at[pair],
                    device_id=(to, gz), device_id_type=MESH,
                ).start()
                return inner

            lax.fori_loop(1, 32, push, 0)

        return carry

    lax.fori_loop(0, J, stage_x, 0)

    channel = (lane // ZC) % 4
    is_depth = channel == 3

    def combine(pair, carry):
        pltpu.make_async_copy(pic_in.at[pair], pic_in.at[pair], recv3.at[pair]).wait()
        before = jnp.zeros((16, 128), F32)
        total = jnp.zeros((16, 128), F32)
        for s in range(32):
            brick = pic_in[pair, s].astype(F32)
            depth = jnp.where(is_depth, brick, 0.0)
            depth = depth + pltpu.roll(depth, 128 - 16, 1)
            depth = depth + pltpu.roll(depth, 128 - 32, 1)
            total = total + jnp.exp(-before) * brick
            before = before + depth
        bricks_ref[pair] = jnp.where(is_depth, 1.0 - jnp.exp(-before), total)
        return carry

    lax.fori_loop(0, 2, combine, 0)

    for chunk in range(J):
        for c in range(3):
            first = sent1.at[chunk, c, pl.ds(0, 3)]
            pltpu.make_async_copy(first, first, send1.at[chunk, c]).wait()
            half_copy(chunk, c).wait_send()
            pltpu.make_async_copy(field.at[chunk, c], field.at[chunk, c], store_sem.at[chunk, c]).wait()

        @pl.when(in_half)
        def _():
            second = sent2.at[chunk, pl.ds(0, 31)]
            pltpu.make_async_copy(second, second, send2.at[chunk]).wait()

        @pl.when(jnp.logical_not(in_half))
        def _():
            pltpu.make_async_copy(sent2.at[chunk], sent2.at[chunk], send2.at[chunk]).wait()

    for pair in range(2):
        third = pic_out.at[pair, pl.ds(0, 31)]
        pltpu.make_async_copy(third, third, send3.at[pair]).wait()


def shards(coeffs):
    table_z, table_y, table_take, table_x = (jnp.asarray(table) for table in tables())
    any_space = pl.BlockSpec(memory_space=pl.ANY)
    current, bricks = pl.pallas_call(
        kernel,
        out_shape=(
            pltpu.VMEM((3, 16, 64, N), F32),
            jax.ShapeDtypeStruct((2, 16, 128), F32),
        ),
        in_specs=[any_space] * 5,
        out_specs=(pl.BlockSpec(memory_space=pltpu.VMEM), pl.BlockSpec(memory_space=pltpu.VMEM)),
        scratch_shapes=[
            pltpu.VMEM((N, N), F32),
            pltpu.VMEM((512 + 2 * SLOTS, N), F32),
            pltpu.VMEM((512, 2 * SLOTS), F32),
            pltpu.VMEM((N, N), F32),
            pltpu.VMEM((24, 128, N), BF),
            pltpu.VMEM((N, N), BF),
            pltpu.VMEM((512 + 2 * SLOTS, N), BF),
            pltpu.VMEM((512, 2 * SLOTS), BF),
            pltpu.VMEM((N, N), BF),
            pltpu.VMEM((J, 3, 4, 2, 8, ZC, 128), BF),
            pltpu.VMEM((J, 3, 4, 2, 8, ZC, 128), BF),
            pltpu.VMEM((J, 3, 2 * SLOTS, 256), BF),
            pltpu.VMEM((J, 3, 2 * SLOTS, 256), BF),
            pltpu.VMEM((J, 32, 3, 2, 16, 128), BF),
            pltpu.VMEM((J, 32, 3, 2, 16, 128), BF),
            pltpu.VMEM((256, N), BF),
            pltpu.VMEM((J, 3, 4, 16 * ZC, 128), F32),
            pltpu.VMEM((128, N), F32),
            pltpu.VMEM((2, 32, 16, 128), BF),
            pltpu.VMEM((2, 32, 16, 128), BF),
            pltpu.SemaphoreType.DMA((5,)),
            pltpu.SemaphoreType.DMA((J, 3)),
            pltpu.SemaphoreType.DMA((J, 3)),
            pltpu.SemaphoreType.DMA((J, 3)),
            pltpu.SemaphoreType.DMA((J, 3)),
            pltpu.SemaphoreType.DMA((J,)),
            pltpu.SemaphoreType.DMA((J,)),
            pltpu.SemaphoreType.DMA((2,)),
            pltpu.SemaphoreType.DMA((2,)),
            pltpu.SemaphoreType.DMA((J, 3)),
        ],
        compiler_params=pltpu.CompilerParams(
            collective_id=0, has_side_effects=True, vmem_limit_bytes=48 * 1024 * 1024
        ),
        name="render",
    )(
        *(
            pltpu.with_memory_space_constraint(operand, pltpu.HBM)
            for operand in (coeffs.reshape(24, 128, N), table_z, table_y, table_take, table_x)
        )
    )
    picture = bricks.reshape(2, 16, 2, 4, ZC).transpose(3, 0, 2, 4, 1).reshape(4, 64, 16)
    return (current, picture)


def solution(mesh):
    return jax.shard_map(
        shards,
        mesh=mesh,
        in_specs=(P(None, "gy", "gz", None),),
        out_specs=(P(None, "gy", "gz", None), P(None, "gz", "gy")),
        check_vma=False,
    )
```

```python
import functools
import math

import jax
import jax.numpy as jnp
import ml_dtypes
import numpy as np
from jax import lax
from jax.experimental import pallas as pl
from jax.experimental.pallas import tpu as pltpu
from jax.sharding import PartitionSpec as P

N = 512
J = 4
ZC = 16
AHEAD = 2
MESH = pl.DeviceIdType.MESH
BF, F32 = jnp.bfloat16, jnp.float32


def make_basis(length):
    mode_index = np.arange(length, dtype=np.int32)[:, None]
    cell_index = np.arange(length, dtype=np.int32)[None, :]
    half_size = length // 2
    frequency = np.where(mode_index <= half_size, mode_index, mode_index - half_size)
    phase_angle = (frequency * cell_index % length).astype(np.float32) * np.float32(2.0 * math.pi / length)
    values = np.where(mode_index <= half_size, np.cos(phase_angle), np.sin(phase_angle)) * np.float32(
        math.sqrt(2.0 / length)
    )
    return values.astype(ml_dtypes.bfloat16)


SLOTS = 136
PAIRS = ((0, 3), (1, 2))


def cells_of(half):
    blocks = [x * 8 + hi * 2 + core for x in range(4) for hi in PAIRS[half] for core in range(2)]
    return np.array([block * 16 + i for block in blocks for i in range(16)])


def slots_of(z_lo, half):
    cells = cells_of(half)
    folded = sorted(set(np.minimum(cells, N - cells).tolist()))
    if z_lo == 1:
        folded = [cell for cell in folded if cell not in (0, N // 2)]
    return folded


def tables():
    basis = make_basis(N).astype(np.float32)
    order_z = np.arange(N).reshape(2, 4, J, ZC).transpose(2, 1, 0, 3).reshape(-1)
    table_z = np.ascontiguousarray(basis.T[order_z])
    keep = np.zeros((4, 2, 256, 4, 2, 64), np.float32)
    give = np.zeros((4, 2, SLOTS, 4, 2, 64), np.float32)
    take = np.zeros((4, 2, 256, 2, SLOTS), np.float32)
    for z_lo in range(2):
        modes = slice(z_lo * 256, z_lo * 256 + 256)
        for half in range(2):
            kind = z_lo * 2 + half
            cells = cells_of(half)
            own = basis[modes, :][:, cells].T.reshape(256, 4, 64)
            slots = slots_of(z_lo, 1 - half)
            sums = np.zeros((SLOTS, 256), np.float32)
            sums[: len(slots)] = basis[modes, :][:, slots].T
            if z_lo == 1:
                sums[:, 0] = 0.0
                sums[len(slots), 0] = basis[256, 0]
            unfold = np.zeros((256, SLOTS), np.float32)
            theirs = slots_of(1 - z_lo, half)
            for row, cell in enumerate(cells):
                folded = min(cell, N - cell)
                if folded in theirs:
                    unfold[row, theirs.index(folded)] = 1.0 if z_lo == 1 or cell < N // 2 else -1.0
                if z_lo == 0:
                    unfold[row, len(theirs)] = 1.0 - 2.0 * (cell % 2)
            for parity in range(2):
                keep[kind, parity, :, :, parity] = own
                give[kind, parity, :, :, parity] = sums.reshape(SLOTS, 4, 64)
                take[kind, parity, :, parity] = unfold
    group, pair, tile = np.meshgrid(np.arange(4), np.arange(8), np.arange(16), indexing="ij")
    slot = group * 16 + tile
    order_x = ((slot // 2) * 16 + pair * 2 + slot % 2).reshape(-1)
    table_x = np.ascontiguousarray(basis[order_x])
    return (
        table_z,
        np.concatenate([keep.reshape(4, 512, 512), give.reshape(4, 2 * SLOTS, 512)], axis=1),
        take.reshape(4, 512, 2 * SLOTS),
        table_x,
    )


def kernel(
    coef_hbm, tz_hbm, ty_hbm, take_hbm, tx_hbm, current_ref, picture_ref,
    raw_z, raw_y, raw_take, raw_x,
    coef, tz, ty, take, tx, sent1, got1, half_out, half_in, sent2, got2, rows_x, field, tint, done, pic_half, pic_near, pic_out, pic_in,
    load_sem, send1, recv1, sendh, recvh, send2, recv2, sendb, recvb, send3, recv3, store_sem,
):
    gy, gz = lax.axis_index("gy"), lax.axis_index("gz")
    at_x, at_hi, at_core = gy // 8, lax.rem(gy // 2, 4), lax.rem(gy, 2)
    at_lo, at_y = gz // 4, lax.rem(gz, 4)
    half = lax.rem(at_lo + at_hi // 2, 2)
    kind = at_lo * 2 + half
    in_half = half == lax.rem((at_hi + 1) // 2, 2)

    def gy_at(step):
        gx = lax.rem(at_x + step // 8, 4)
        gh = lax.rem(at_hi + lax.rem(step // 2, 4), 4)
        gc = lax.rem(at_core + step, 2)
        return gx * 8 + gh * 2 + gc

    def y_at(step):
        return at_lo * 4 + lax.rem(at_y + step, 4)

    twin = (1 - at_lo) * 4 + at_y

    barrier = pltpu.get_barrier_semaphore()

    def greet(step, carry):
        to = gy_at(step)
        pl.semaphore_signal(barrier, inc=1, device_id=(to, gz), device_id_type=MESH)
        pl.semaphore_signal(barrier, inc=1, device_id=(to, twin), device_id_type=MESH)
        return carry

    loads = [
        pltpu.make_async_copy(tz_hbm, raw_z, load_sem.at[0]),
        pltpu.make_async_copy(coef_hbm.at[pl.ds(0, 8)], coef.at[pl.ds(0, 8)], load_sem.at[1]),
        pltpu.make_async_copy(coef_hbm.at[pl.ds(8, 16)], coef.at[pl.ds(8, 16)], load_sem.at[5]),
        pltpu.make_async_copy(ty_hbm.at[kind], raw_y, load_sem.at[2]),
        pltpu.make_async_copy(take_hbm.at[kind], raw_take, load_sem.at[3]),
        pltpu.make_async_copy(tx_hbm, raw_x, load_sem.at[4]),
    ]
    loads[0].start()
    loads[1].start()
    for step in range(1, 4):
        pl.semaphore_signal(barrier, inc=1, device_id=(gy, y_at(step)), device_id_type=MESH)
    pl.semaphore_signal(barrier, inc=1, device_id=(gy, twin), device_id_type=MESH)
    lax.fori_loop(1, 32, greet, 0)
    for load in loads[2:]:
        load.start()
    loads[0].wait()
    tz[...] = raw_z[...].astype(BF)
    loads[1].wait()

    def transform_z(unit):
        chunk, c = unit // 3, lax.rem(unit, 3)

        def one(p, carry):
            out = lax.dot_general(
                tz[pl.ds(pl.multiple_of(chunk * 128, 128), 128), :], coef[c * 8 + p], (((1,), (1,)), ((), ())),
                preferred_element_type=F32,
            ).astype(BF)
            for y in range(4):
                for lo in range(2):
                    row = (y * 2 + lo) * ZC
                    sent1[chunk, c, y, lo, p] = out[row : row + ZC]
            return carry

        lax.fori_loop(0, 8, one, 0, unroll=4)

    def send_z(unit):
        chunk, c = unit // 3, lax.rem(unit, 3)
        pltpu.make_async_copy(sent1.at[chunk, c, at_y], got1.at[chunk, c, at_y], recv1.at[chunk, c]).start()
        for step in range(1, 4):
            to = lax.rem(at_y + step, 4)
            pltpu.make_async_remote_copy(
                src_ref=sent1.at[chunk, c, to], dst_ref=got1.at[chunk, c, at_y],
                send_sem=send1.at[chunk, c], recv_sem=recv1.at[chunk, c],
                device_id=(gy, at_lo * 4 + to), device_id_type=MESH,
            ).start()

    transform_z(0)
    pl.semaphore_wait(barrier, 66)
    send_z(0)
    loads[2].wait()
    for unit in range(1, AHEAD):
        transform_z(unit)
        send_z(unit)
    loads[3].wait()
    loads[4].wait()
    loads[5].wait()
    ty[...] = raw_y[...].astype(BF)
    take[...] = raw_take[...].astype(BF)
    tx[...] = raw_x[...].astype(BF)

    def rows_of(chunk, c):
        return jnp.concatenate([got1[chunk, c, s].reshape(256, 128) for s in range(4)], axis=1)

    def half_copy(chunk, c):
        return pltpu.make_async_remote_copy(
            src_ref=half_out.at[chunk, c], dst_ref=half_in.at[chunk, c],
            send_sem=sendh.at[chunk, c], recv_sem=recvh.at[chunk, c],
            device_id=(gy, twin), device_id_type=MESH,
        )

    def push_y(chunk):
        def push(step, carry):
            to_x = lax.rem(at_x + step // 8, 4)
            place = lax.rem(step // 4 + at_hi, 2)
            to_hi = jnp.where(half == 0, 3 * place, 1 + place)
            to_lo = lax.rem(step // 2 + at_lo, 2)
            to_core = lax.rem(step + at_core, 2)
            slot = (to_x * 4 + place * 2 + to_core) * 2 + to_lo
            to = to_x * 8 + to_hi * 2 + to_core
            same = jnp.logical_and(to == gy, to_lo == at_lo)
            source, target = sent2.at[chunk, slot], got2.at[chunk, gy]

            @pl.when(same)
            def _():
                pltpu.make_async_copy(source, target, recv2.at[chunk]).start()

            @pl.when(jnp.logical_not(same))
            def _():
                pltpu.make_async_remote_copy(
                    src_ref=source, dst_ref=target,
                    send_sem=send2.at[chunk], recv_sem=recv2.at[chunk],
                    device_id=(to, to_lo * 4 + at_y), device_id_type=MESH,
                ).start()

            return carry

        lax.fori_loop(0, 32, push, 0)

    def stage_y(unit, carry):
        @pl.when(unit < 3 * J)
        def _():
            chunk, c = unit // 3, lax.rem(unit, 3)
            pltpu.make_async_copy(got1.at[chunk, c], got1.at[chunk, c], recv1.at[chunk, c]).wait()
            half_out[chunk, c] = lax.dot_general(
                ty[512:, :], rows_of(chunk, c), (((1,), (1,)), ((), ())), preferred_element_type=F32
            ).astype(BF)
            half_copy(chunk, c).start()

        @pl.when(unit + AHEAD < 3 * J)
        def _():
            transform_z(unit + AHEAD)
            send_z(unit + AHEAD)

        @pl.when(unit >= 1)
        def _():
            chunk, c = (unit - 1) // 3, lax.rem(unit - 1, 3)
            half_copy(chunk, c).wait_recv()
            rows = rows_of(chunk, c)
            theirs = half_in[chunk, c]
            for parity in range(2):
                out = lax.dot_general(
                    ty[parity * 256 : parity * 256 + 256, :], rows, (((1,), (1,)), ((), ())), preferred_element_type=F32
                )
                out = out + jnp.dot(
                    take[parity * 256 : parity * 256 + 256, :], theirs, preferred_element_type=F32
                )
                out = out.astype(BF)
                for d in range(16):
                    for lo in range(2):
                        sent2[chunk, d * 2 + lo, c, parity] = out[d * 16 : d * 16 + 16, lo * 128 : lo * 128 + 128]

            @pl.when(c == 2)
            def _():
                push_y(chunk)

        return carry

    lax.fori_loop(0, 3 * J + 1, stage_y, 0)

    lane = lax.broadcasted_iota(jnp.int32, (16, 128), 1)

    channel = (lane // ZC) % 4
    is_depth = channel == 3

    sibling = gy + 1 - 2 * at_core

    def sibling_copy(pair):
        return pltpu.make_async_remote_copy(
            src_ref=pic_half.at[pair, 1 - at_core], dst_ref=pic_near.at[pair],
            send_sem=sendb.at[pair], recv_sem=recvb.at[pair],
            device_id=(sibling, gz), device_id_type=MESH,
        )

    def spread_depth(brick):
        depth = jnp.where(is_depth, brick, 0.0)
        depth = depth + pltpu.roll(depth, 128 - 16, 1)
        return depth + pltpu.roll(depth, 128 - 32, 1)

    def send_pair(pair):
        sibling_copy(pair).wait_recv()
        for m in range(16):
            mine = pic_half[pair, at_core, m].astype(F32)
            theirs = pic_near[pair, m].astype(F32)
            front = jnp.where(at_core == 0, mine, theirs)
            back = jnp.where(at_core == 0, theirs, mine)
            passed = jnp.where(is_depth, 1.0, jnp.exp(-spread_depth(front)))
            pic_out[pair, m] = (front + passed * back).astype(BF)
        here = gy // 2
        pltpu.make_async_copy(pic_out.at[pair, here], pic_in.at[pair, here], recv3.at[pair]).start()

        def push(step, inner):
            to = lax.rem(here // 4 + step // 4, 4) * 4 + lax.rem(here + step, 4)
            pltpu.make_async_remote_copy(
                src_ref=pic_out.at[pair, to], dst_ref=pic_in.at[pair, here],
                send_sem=send3.at[pair], recv_sem=recv3.at[pair],
                device_id=(to * 2 + at_core, gz), device_id_type=MESH,
            ).start()
            return inner

        lax.fori_loop(1, 16, push, 0)

    def combine(pair):
        pltpu.make_async_copy(pic_in.at[pair], pic_in.at[pair], recv3.at[pair]).wait()
        before = jnp.zeros((16, 128), F32)
        total = jnp.zeros((16, 128), F32)
        for m in range(16):
            brick = pic_in[pair, m].astype(F32)
            total = total + jnp.exp(-before) * brick
            before = before + spread_depth(brick)
        done[pl.ds(pair * 16, 16), :] = jnp.where(is_depth, 1.0 - jnp.exp(-before), total)

    def stage_x(chunk, carry):
        @pl.when(chunk == 2)
        def _():
            send_pair(0)

        @pl.when(chunk == J - 1)
        def _():
            combine(0)

        pltpu.make_async_copy(got2.at[chunk], got2.at[chunk], recv2.at[chunk]).wait()

        def component(c, inner):
            for group in range(4):
                tiles = [got2[chunk, group * 8 + t // 2, c, t % 2].astype(F32) for t in range(16)]
                for bit in (1, 2, 4, 8):
                    low = (lane & bit) == 0
                    for t in range(16):
                        if t & bit == 0:
                            u, v = tiles[t], tiles[t + bit]
                            tiles[t] = jnp.where(low, u, pltpu.roll(v, bit, 1))
                            tiles[t + bit] = jnp.where(low, pltpu.roll(u, 128 - bit, 1), v)
                for t in range(16):
                    rows_x[pl.ds(t * 16, 16), pl.ds(group * 128, 128)] = tiles[t].astype(BF)
            out = jnp.dot(rows_x[...], tx[...], preferred_element_type=F32)
            for col in range(4):
                for t in range(16):
                    field[chunk, c, col, pl.ds(t, 16, stride=ZC), :] = out[
                        t * 16 : (t + 1) * 16, col * 128 : (col + 1) * 128
                    ]
                pltpu.make_async_copy(
                    field.at[chunk, c, col].reshape(16, ZC, 128),
                    current_ref.at[c, :, pl.ds(chunk * ZC, ZC), pl.ds(col * 128, 128)],
                    store_sem.at[chunk, c],
                ).start()
            return inner

        lax.fori_loop(0, 3, component, 0)
        absorb = 0.6 / N
        for col in range(4):
            cols = pl.ds(col * 128, 128)
            passed = jnp.ones((ZC, 128), F32)
            depth = jnp.zeros((ZC, 128), F32)
            colors = [jnp.zeros((ZC, 128), F32)] * 3
            for y in range(16):
                parts = [field[chunk, c, col, pl.ds(y * ZC, ZC), :] for c in range(3)]
                density = parts[0] * parts[0] + parts[1] * parts[1] + parts[2] * parts[2]
                optical = absorb * density
                left = jnp.exp(-optical)
                weight = 4.0 * (passed * (1.0 - left))
                passed = passed * left
                depth = depth + optical
                levels = (
                    jnp.clip((density - 2.0) * (1.0 / 3.0), 0.0, 1.0),
                    jnp.clip(1.0 - jnp.abs(density - 3.0) * 0.5, 0.0, 1.0),
                    jnp.clip(1.0 - density * 0.5, 0.0, 1.0),
                )
                colors = [color + weight * level for color, level in zip(colors, levels)]
            part = lax.rem(chunk, 2)
            for k, value in enumerate(colors + [depth]):
                tint[pl.ds(part * 64 + k * ZC, ZC), cols] = value

        @pl.when(lax.rem(chunk, 2) == 1)
        def _():
            pair = chunk // 2
            for col in range(4):
                turned = jnp.transpose(tint[:, col * 128 : (col + 1) * 128]).astype(BF)
                for g in range(8):
                    pic_half[pair, g % 2, col * 4 + g // 2] = turned[g * 16 : (g + 1) * 16]
            sibling_copy(pair).start()

        return carry

    lax.fori_loop(0, J, stage_x, 0)

    send_pair(1)
    combine(1)
    for pair in range(2):
        for part in range(2):
            for k in range(4):
                start, place = (part * 4 + k) * ZC, (pair * 2 + part) * ZC
                picture_ref[k, :, place : place + ZC] = done[pair * 16 : pair * 16 + 16, start : start + ZC]

    for chunk in range(J):
        for c in range(3):
            first = sent1.at[chunk, c, pl.ds(0, 3)]
            pltpu.make_async_copy(first, first, send1.at[chunk, c]).wait()
            half_copy(chunk, c).wait_send()
            pltpu.make_async_copy(field.at[chunk, c], field.at[chunk, c], store_sem.at[chunk, c]).wait()

        @pl.when(in_half)
        def _():
            second = sent2.at[chunk, pl.ds(0, 31)]
            pltpu.make_async_copy(second, second, send2.at[chunk]).wait()

        @pl.when(jnp.logical_not(in_half))
        def _():
            pltpu.make_async_copy(sent2.at[chunk], sent2.at[chunk], send2.at[chunk]).wait()

    for pair in range(2):
        sibling_copy(pair).wait_send()
        third = pic_out.at[pair, pl.ds(0, 15)]
        pltpu.make_async_copy(third, third, send3.at[pair]).wait()


def shards(coeffs):
    table_z, table_y, table_take, table_x = (jnp.asarray(table) for table in tables())
    any_space = pl.BlockSpec(memory_space=pl.ANY)
    current, picture = pl.pallas_call(
        kernel,
        out_shape=(
            pltpu.VMEM((3, 16, 64, N), F32),
            pltpu.VMEM((4, 16, 64), F32),
        ),
        in_specs=[any_space] * 5,
        out_specs=(pl.BlockSpec(memory_space=pltpu.VMEM), pl.BlockSpec(memory_space=pltpu.VMEM)),
        scratch_shapes=[
            pltpu.VMEM((N, N), F32),
            pltpu.VMEM((512 + 2 * SLOTS, N), F32),
            pltpu.VMEM((512, 2 * SLOTS), F32),
            pltpu.VMEM((N, N), F32),
            pltpu.VMEM((24, 128, N), BF),
            pltpu.VMEM((N, N), BF),
            pltpu.VMEM((512 + 2 * SLOTS, N), BF),
            pltpu.VMEM((512, 2 * SLOTS), BF),
            pltpu.VMEM((N, N), BF),
            pltpu.VMEM((J, 3, 4, 2, 8, ZC, 128), BF),
            pltpu.VMEM((J, 3, 4, 2, 8, ZC, 128), BF),
            pltpu.VMEM((J, 3, 2 * SLOTS, 256), BF),
            pltpu.VMEM((J, 3, 2 * SLOTS, 256), BF),
            pltpu.VMEM((J, 32, 3, 2, 16, 128), BF),
            pltpu.VMEM((J, 32, 3, 2, 16, 128), BF),
            pltpu.VMEM((256, N), BF),
            pltpu.VMEM((J, 3, 4, 16 * ZC, 128), F32),
            pltpu.VMEM((128, N), F32),
            pltpu.VMEM((32, 128), F32),
            pltpu.VMEM((2, 2, 16, 16, 128), BF),
            pltpu.VMEM((2, 16, 16, 128), BF),
            pltpu.VMEM((2, 16, 16, 128), BF),
            pltpu.VMEM((2, 16, 16, 128), BF),
            pltpu.SemaphoreType.DMA((6,)),
            pltpu.SemaphoreType.DMA((J, 3)),
            pltpu.SemaphoreType.DMA((J, 3)),
            pltpu.SemaphoreType.DMA((J, 3)),
            pltpu.SemaphoreType.DMA((J, 3)),
            pltpu.SemaphoreType.DMA((J,)),
            pltpu.SemaphoreType.DMA((J,)),
            pltpu.SemaphoreType.DMA((2,)),
            pltpu.SemaphoreType.DMA((2,)),
            pltpu.SemaphoreType.DMA((2,)),
            pltpu.SemaphoreType.DMA((2,)),
            pltpu.SemaphoreType.DMA((J, 3)),
        ],
        compiler_params=pltpu.CompilerParams(
            collective_id=0, has_side_effects=True, vmem_limit_bytes=48 * 1024 * 1024
        ),
        name="render",
    )(
        *(
            pltpu.with_memory_space_constraint(operand, pltpu.HBM)
            for operand in (coeffs.reshape(24, 128, N), table_z, table_y, table_take, table_x)
        )
    )
    return (current, picture.transpose(0, 2, 1))


def solution(mesh):
    return jax.shard_map(
        shards,
        mesh=mesh,
        in_specs=(P(None, "gy", "gz", None),),
        out_specs=(P(None, "gy", "gz", None), P(None, "gz", "gy")),
        check_vma=False,
    )
```

```python
import functools
import math

import jax
import jax.numpy as jnp
import ml_dtypes
import numpy as np
from jax import lax
from jax.experimental import pallas as pl
from jax.experimental.pallas import tpu as pltpu
from jax.sharding import PartitionSpec as P

N = 512
J = 4
ZC = 16
AHEAD = 2
MESH = pl.DeviceIdType.MESH
BF, F32 = jnp.bfloat16, jnp.float32


def make_basis(length):
    mode_index = np.arange(length, dtype=np.int32)[:, None]
    cell_index = np.arange(length, dtype=np.int32)[None, :]
    half_size = length // 2
    frequency = np.where(mode_index <= half_size, mode_index, mode_index - half_size)
    phase_angle = (frequency * cell_index % length).astype(np.float32) * np.float32(2.0 * math.pi / length)
    values = np.where(mode_index <= half_size, np.cos(phase_angle), np.sin(phase_angle)) * np.float32(
        math.sqrt(2.0 / length)
    )
    return values.astype(ml_dtypes.bfloat16)


SLOTS = 136
PAIRS = ((0, 3), (1, 2))


def cells_of(half):
    blocks = [x * 8 + hi * 2 + core for x in range(4) for hi in PAIRS[half] for core in range(2)]
    return np.array([block * 16 + i for block in blocks for i in range(16)])


def slots_of(z_lo, half):
    cells = cells_of(half)
    folded = sorted(set(np.minimum(cells, N - cells).tolist()))
    if z_lo == 1:
        folded = [cell for cell in folded if cell not in (0, N // 2)]
    return folded


def tables():
    basis = make_basis(N).astype(np.float32)
    order_z = np.arange(N).reshape(2, 4, J, ZC).transpose(2, 1, 0, 3).reshape(-1)
    table_z = np.ascontiguousarray(basis.T[order_z])
    keep = np.zeros((4, 2, 256, 4, 2, 64), np.float32)
    give = np.zeros((4, 2, SLOTS, 4, 2, 64), np.float32)
    take = np.zeros((4, 2, 256, 2, SLOTS), np.float32)
    for z_lo in range(2):
        modes = slice(z_lo * 256, z_lo * 256 + 256)
        for half in range(2):
            kind = z_lo * 2 + half
            cells = cells_of(half)
            own = basis[modes, :][:, cells].T.reshape(256, 4, 64)
            slots = slots_of(z_lo, 1 - half)
            sums = np.zeros((SLOTS, 256), np.float32)
            sums[: len(slots)] = basis[modes, :][:, slots].T
            if z_lo == 1:
                sums[:, 0] = 0.0
                sums[len(slots), 0] = basis[256, 0]
            unfold = np.zeros((256, SLOTS), np.float32)
            theirs = slots_of(1 - z_lo, half)
            for row, cell in enumerate(cells):
                folded = min(cell, N - cell)
                if folded in theirs:
                    unfold[row, theirs.index(folded)] = 1.0 if z_lo == 1 or cell < N // 2 else -1.0
                if z_lo == 0:
                    unfold[row, len(theirs)] = 1.0 - 2.0 * (cell % 2)
            for parity in range(2):
                keep[kind, parity, :, :, parity] = own
                give[kind, parity, :, :, parity] = sums.reshape(SLOTS, 4, 64)
                take[kind, parity, :, parity] = unfold
    group, pair, tile = np.meshgrid(np.arange(4), np.arange(8), np.arange(16), indexing="ij")
    slot = group * 16 + tile
    order_x = ((slot // 2) * 16 + pair * 2 + slot % 2).reshape(-1)
    table_x = np.ascontiguousarray(basis[order_x])
    return (
        table_z,
        np.concatenate([keep.reshape(4, 512, 512), give.reshape(4, 2 * SLOTS, 512)], axis=1),
        take.reshape(4, 512, 2 * SLOTS),
        table_x,
    )


def kernel(
    coef_hbm, tz_hbm, ty_hbm, take_hbm, tx_hbm, current_ref, picture_ref,
    raw_z, raw_y, raw_take, raw_x,
    coef, tz, ty, take, tx, sent1, got1, half_out, half_in, sent2, got2, rows_x, field, tint, done, pic_half, pic_near, pic_out, pic_in,
    load_sem, send1, recv1, sendh, recvh, send2, recv2, sendb, recvb, send3, recv3, store_sem,
):
    gy, gz = lax.axis_index("gy"), lax.axis_index("gz")
    at_x, at_hi, at_core = gy // 8, lax.rem(gy // 2, 4), lax.rem(gy, 2)
    at_lo, at_y = gz // 4, lax.rem(gz, 4)
    half = lax.rem(at_lo + at_hi // 2, 2)
    kind = at_lo * 2 + half
    in_half = half == lax.rem((at_hi + 1) // 2, 2)

    def gy_at(step):
        gx = lax.rem(at_x + step // 8, 4)
        gh = lax.rem(at_hi + lax.rem(step // 2, 4), 4)
        gc = lax.rem(at_core + step, 2)
        return gx * 8 + gh * 2 + gc

    def y_at(step):
        return at_lo * 4 + lax.rem(at_y + step, 4)

    twin = (1 - at_lo) * 4 + at_y

    barrier = pltpu.get_barrier_semaphore()

    def greet(step, carry):
        to = gy_at(step)
        pl.semaphore_signal(barrier, inc=1, device_id=(to, gz), device_id_type=MESH)
        pl.semaphore_signal(barrier, inc=1, device_id=(to, twin), device_id_type=MESH)
        return carry

    loads = [
        pltpu.make_async_copy(tz_hbm, raw_z, load_sem.at[0]),
        pltpu.make_async_copy(coef_hbm.at[pl.ds(0, 8)], coef.at[pl.ds(0, 8)], load_sem.at[1]),
        pltpu.make_async_copy(coef_hbm.at[pl.ds(8, 16)], coef.at[pl.ds(8, 16)], load_sem.at[5]),
        pltpu.make_async_copy(ty_hbm.at[kind], raw_y, load_sem.at[2]),
        pltpu.make_async_copy(take_hbm.at[kind], raw_take, load_sem.at[3]),
        pltpu.make_async_copy(tx_hbm, raw_x, load_sem.at[4]),
    ]
    loads[0].start()
    loads[1].start()
    for step in range(1, 4):
        pl.semaphore_signal(barrier, inc=1, device_id=(gy, y_at(step)), device_id_type=MESH)
    pl.semaphore_signal(barrier, inc=1, device_id=(gy, twin), device_id_type=MESH)
    lax.fori_loop(1, 32, greet, 0)
    for load in loads[2:]:
        load.start()
    loads[0].wait()
    tz[...] = raw_z[...].astype(BF)
    loads[1].wait()

    def transform_z(unit):
        chunk, c = unit // 3, lax.rem(unit, 3)

        def one(p, carry):
            out = lax.dot_general(
                tz[pl.ds(pl.multiple_of(chunk * 128, 128), 128), :], coef[c * 8 + p], (((1,), (1,)), ((), ())),
                preferred_element_type=F32,
            ).astype(BF)
            for y in range(4):
                for lo in range(2):
                    row = (y * 2 + lo) * ZC
                    sent1[chunk, c, y, lo, p] = out[row : row + ZC]
            return carry

        lax.fori_loop(0, 8, one, 0, unroll=4)

    def send_z(unit):
        chunk, c = unit // 3, lax.rem(unit, 3)
        pltpu.make_async_copy(sent1.at[chunk, c, at_y], got1.at[chunk, c, at_y], recv1.at[chunk, c]).start()
        for step in range(1, 4):
            to = lax.rem(at_y + step, 4)
            pltpu.make_async_remote_copy(
                src_ref=sent1.at[chunk, c, to], dst_ref=got1.at[chunk, c, at_y],
                send_sem=send1.at[chunk, c], recv_sem=recv1.at[chunk, c],
                device_id=(gy, at_lo * 4 + to), device_id_type=MESH,
            ).start()

    transform_z(0)
    pl.semaphore_wait(barrier, 66)
    send_z(0)
    loads[2].wait()
    for unit in range(1, AHEAD):
        transform_z(unit)
        send_z(unit)
    loads[3].wait()
    loads[4].wait()
    loads[5].wait()
    ty[...] = raw_y[...].astype(BF)
    take[...] = raw_take[...].astype(BF)
    tx[...] = raw_x[...].astype(BF)

    def rows_of(chunk, c):
        return jnp.concatenate([got1[chunk, c, s].reshape(256, 128) for s in range(4)], axis=1)

    def half_copy(chunk, c):
        return pltpu.make_async_remote_copy(
            src_ref=half_out.at[chunk, c], dst_ref=half_in.at[chunk, c],
            send_sem=sendh.at[chunk, c], recv_sem=recvh.at[chunk, c],
            device_id=(gy, twin), device_id_type=MESH,
        )

    def push_y(chunk, first, count):
        def push(step, carry):
            to_x = lax.rem(at_x + step // 8, 4)
            place = lax.rem(step // 4 + at_hi, 2)
            to_hi = jnp.where(half == 0, 3 * place, 1 + place)
            to_lo = lax.rem(step // 2 + at_lo, 2)
            to_core = lax.rem(step + at_core, 2)
            slot = (to_x * 4 + place * 2 + to_core) * 2 + to_lo
            to = to_x * 8 + to_hi * 2 + to_core
            same = jnp.logical_and(to == gy, to_lo == at_lo)
            picked = pl.ds(first, count)
            source, target = sent2.at[chunk, slot, picked], got2.at[chunk, gy, picked]

            @pl.when(same)
            def _():
                pltpu.make_async_copy(source, target, recv2.at[chunk]).start()

            @pl.when(jnp.logical_not(same))
            def _():
                pltpu.make_async_remote_copy(
                    src_ref=source, dst_ref=target,
                    send_sem=send2.at[chunk], recv_sem=recv2.at[chunk],
                    device_id=(to, to_lo * 4 + at_y), device_id_type=MESH,
                ).start()

            return carry

        lax.fori_loop(0, 32, push, 0)

    def stage_y(unit, carry):
        @pl.when(unit < 3 * J)
        def _():
            chunk, c = unit // 3, lax.rem(unit, 3)
            pltpu.make_async_copy(got1.at[chunk, c], got1.at[chunk, c], recv1.at[chunk, c]).wait()
            half_out[chunk, c] = lax.dot_general(
                ty[512:, :], rows_of(chunk, c), (((1,), (1,)), ((), ())), preferred_element_type=F32
            ).astype(BF)
            half_copy(chunk, c).start()

        @pl.when(unit + AHEAD < 3 * J)
        def _():
            transform_z(unit + AHEAD)
            send_z(unit + AHEAD)

        @pl.when(unit >= 1)
        def _():
            chunk, c = (unit - 1) // 3, lax.rem(unit - 1, 3)
            half_copy(chunk, c).wait_recv()
            rows = rows_of(chunk, c)
            theirs = half_in[chunk, c]
            for parity in range(2):
                out = lax.dot_general(
                    ty[parity * 256 : parity * 256 + 256, :], rows, (((1,), (1,)), ((), ())), preferred_element_type=F32
                )
                out = out + jnp.dot(
                    take[parity * 256 : parity * 256 + 256, :], theirs, preferred_element_type=F32
                )
                out = out.astype(BF)
                for d in range(16):
                    for lo in range(2):
                        sent2[chunk, d * 2 + lo, c, parity] = out[d * 16 : d * 16 + 16, lo * 128 : lo * 128 + 128]

            @pl.when(jnp.logical_and(chunk == J - 1, c == 1))
            def _():
                push_y(chunk, 0, 2)

            @pl.when(jnp.logical_and(chunk == J - 1, c == 2))
            def _():
                push_y(chunk, 2, 1)

            @pl.when(jnp.logical_and(chunk < J - 1, c == 2))
            def _():
                push_y(chunk, 0, 3)

        return carry

    lax.fori_loop(0, 3 * J + 1, stage_y, 0)

    lane = lax.broadcasted_iota(jnp.int32, (16, 128), 1)

    channel = (lane // ZC) % 4
    is_depth = channel == 3

    sibling = gy + 1 - 2 * at_core

    def sibling_copy(pair):
        return pltpu.make_async_remote_copy(
            src_ref=pic_half.at[pair, 1 - at_core], dst_ref=pic_near.at[pair],
            send_sem=sendb.at[pair], recv_sem=recvb.at[pair],
            device_id=(sibling, gz), device_id_type=MESH,
        )

    def spread_depth(brick):
        depth = jnp.where(is_depth, brick, 0.0)
        depth = depth + pltpu.roll(depth, 128 - 16, 1)
        return depth + pltpu.roll(depth, 128 - 32, 1)

    def send_pair(pair):
        sibling_copy(pair).wait_recv()
        for m in range(16):
            mine = pic_half[pair, at_core, m].astype(F32)
            theirs = pic_near[pair, m].astype(F32)
            front = jnp.where(at_core == 0, mine, theirs)
            back = jnp.where(at_core == 0, theirs, mine)
            passed = jnp.where(is_depth, 1.0, jnp.exp(-spread_depth(front)))
            pic_out[pair, m] = (front + passed * back).astype(BF)
        here = gy // 2
        pltpu.make_async_copy(pic_out.at[pair, here], pic_in.at[pair, here], recv3.at[pair]).start()

        def push(step, inner):
            to = lax.rem(here // 4 + step // 4, 4) * 4 + lax.rem(here + step, 4)
            pltpu.make_async_remote_copy(
                src_ref=pic_out.at[pair, to], dst_ref=pic_in.at[pair, here],
                send_sem=send3.at[pair], recv_sem=recv3.at[pair],
                device_id=(to * 2 + at_core, gz), device_id_type=MESH,
            ).start()
            return inner

        lax.fori_loop(1, 16, push, 0)

    def combine(pair):
        pltpu.make_async_copy(pic_in.at[pair], pic_in.at[pair], recv3.at[pair]).wait()
        before = jnp.zeros((16, 128), F32)
        total = jnp.zeros((16, 128), F32)
        for m in range(16):
            brick = pic_in[pair, m].astype(F32)
            total = total + jnp.exp(-before) * brick
            before = before + spread_depth(brick)
        done[pl.ds(pair * 16, 16), :] = jnp.where(is_depth, 1.0 - jnp.exp(-before), total)

    def stage_x(chunk, carry):
        @pl.when(chunk == 2)
        def _():
            send_pair(0)

        @pl.when(chunk == J - 1)
        def _():
            combine(0)

        pltpu.make_async_copy(got2.at[chunk], got2.at[chunk], recv2.at[chunk]).wait()

        def component(c, inner):
            for group in range(4):
                tiles = [got2[chunk, group * 8 + t // 2, c, t % 2] for t in range(16)]
                for bit in (1, 2, 4, 8):
                    low = (lane & bit) == 0
                    for t in range(16):
                        if t & bit == 0:
                            u, v = tiles[t], tiles[t + bit]
                            tiles[t] = jnp.where(low, u, pltpu.roll(v, bit, 1))
                            tiles[t + bit] = jnp.where(low, pltpu.roll(u, 128 - bit, 1), v)
                for t in range(16):
                    rows_x[pl.ds(t * 16, 16), pl.ds(group * 128, 128)] = tiles[t]
            out = jnp.dot(rows_x[...], tx[...], preferred_element_type=F32)
            for col in range(4):
                for t in range(16):
                    field[chunk, c, col, pl.ds(t, 16, stride=ZC), :] = out[
                        t * 16 : (t + 1) * 16, col * 128 : (col + 1) * 128
                    ]
                pltpu.make_async_copy(
                    field.at[chunk, c, col].reshape(16, ZC, 128),
                    current_ref.at[c, :, pl.ds(chunk * ZC, ZC), pl.ds(col * 128, 128)],
                    store_sem.at[chunk, c],
                ).start()
            return inner

        lax.fori_loop(0, 3, component, 0)
        absorb = 0.6 / N
        for col in range(4):
            cols = pl.ds(col * 128, 128)
            passed = jnp.ones((ZC, 128), F32)
            depth = jnp.zeros((ZC, 128), F32)
            colors = [jnp.zeros((ZC, 128), F32)] * 3
            for y in range(16):
                parts = [field[chunk, c, col, pl.ds(y * ZC, ZC), :] for c in range(3)]
                density = parts[0] * parts[0] + parts[1] * parts[1] + parts[2] * parts[2]
                optical = absorb * density
                left = jnp.exp(-optical)
                weight = 4.0 * (passed * (1.0 - left))
                passed = passed * left
                depth = depth + optical
                levels = (
                    jnp.clip((density - 2.0) * (1.0 / 3.0), 0.0, 1.0),
                    jnp.clip(1.0 - jnp.abs(density - 3.0) * 0.5, 0.0, 1.0),
                    jnp.clip(1.0 - density * 0.5, 0.0, 1.0),
                )
                colors = [color + weight * level for color, level in zip(colors, levels)]
            part = lax.rem(chunk, 2)
            for k, value in enumerate(colors + [depth]):
                tint[pl.ds(part * 64 + k * ZC, ZC), cols] = value

        @pl.when(lax.rem(chunk, 2) == 1)
        def _():
            pair = chunk // 2
            for col in range(4):
                turned = jnp.transpose(tint[:, col * 128 : (col + 1) * 128]).astype(BF)
                for g in range(8):
                    pic_half[pair, g % 2, col * 4 + g // 2] = turned[g * 16 : (g + 1) * 16]
            sibling_copy(pair).start()

        return carry

    lax.fori_loop(0, J, stage_x, 0)

    send_pair(1)
    combine(1)
    for pair in range(2):
        for part in range(2):
            for k in range(4):
                start, place = (part * 4 + k) * ZC, (pair * 2 + part) * ZC
                picture_ref[k, :, place : place + ZC] = done[pair * 16 : pair * 16 + 16, start : start + ZC]

    for chunk in range(J):
        for c in range(3):
            first = sent1.at[chunk, c, pl.ds(0, 3)]
            pltpu.make_async_copy(first, first, send1.at[chunk, c]).wait()
            half_copy(chunk, c).wait_send()
            pltpu.make_async_copy(field.at[chunk, c], field.at[chunk, c], store_sem.at[chunk, c]).wait()

        @pl.when(in_half)
        def _():
            second = sent2.at[chunk, pl.ds(0, 31)]
            pltpu.make_async_copy(second, second, send2.at[chunk]).wait()

        @pl.when(jnp.logical_not(in_half))
        def _():
            pltpu.make_async_copy(sent2.at[chunk], sent2.at[chunk], send2.at[chunk]).wait()

    for pair in range(2):
        sibling_copy(pair).wait_send()
        third = pic_out.at[pair, pl.ds(0, 15)]
        pltpu.make_async_copy(third, third, send3.at[pair]).wait()


def write_out(current_ref, picture_ref, current_hbm, picture_hbm, sems):
    copies = [pltpu.make_async_copy(picture_ref, picture_hbm, sems.at[12])]
    for c in range(3):
        for part in range(4):
            rows = pl.ds(part * 4, 4)
            copies.append(
                pltpu.make_async_copy(current_ref.at[c, rows], current_hbm.at[c, rows], sems.at[c * 4 + part])
            )
    for copy in copies:
        copy.start()
    for copy in copies:
        copy.wait()


def shards(coeffs):
    table_z, table_y, table_take, table_x = (jnp.asarray(table) for table in tables())
    any_space = pl.BlockSpec(memory_space=pl.ANY)
    current, picture = pl.pallas_call(
        kernel,
        out_shape=(
            pltpu.VMEM((3, 16, 64, N), F32),
            pltpu.VMEM((4, 16, 64), F32),
        ),
        in_specs=[any_space] * 5,
        out_specs=(pl.BlockSpec(memory_space=pltpu.VMEM), pl.BlockSpec(memory_space=pltpu.VMEM)),
        scratch_shapes=[
            pltpu.VMEM((N, N), F32),
            pltpu.VMEM((512 + 2 * SLOTS, N), F32),
            pltpu.VMEM((512, 2 * SLOTS), F32),
            pltpu.VMEM((N, N), F32),
            pltpu.VMEM((24, 128, N), BF),
            pltpu.VMEM((N, N), BF),
            pltpu.VMEM((512 + 2 * SLOTS, N), BF),
            pltpu.VMEM((512, 2 * SLOTS), BF),
            pltpu.VMEM((N, N), BF),
            pltpu.VMEM((J, 3, 4, 2, 8, ZC, 128), BF),
            pltpu.VMEM((J, 3, 4, 2, 8, ZC, 128), BF),
            pltpu.VMEM((J, 3, 2 * SLOTS, 256), BF),
            pltpu.VMEM((J, 3, 2 * SLOTS, 256), BF),
            pltpu.VMEM((J, 32, 3, 2, 16, 128), BF),
            pltpu.VMEM((J, 32, 3, 2, 16, 128), BF),
            pltpu.VMEM((256, N), BF),
            pltpu.VMEM((J, 3, 4, 16 * ZC, 128), F32),
            pltpu.VMEM((128, N), F32),
            pltpu.VMEM((32, 128), F32),
            pltpu.VMEM((2, 2, 16, 16, 128), BF),
            pltpu.VMEM((2, 16, 16, 128), BF),
            pltpu.VMEM((2, 16, 16, 128), BF),
            pltpu.VMEM((2, 16, 16, 128), BF),
            pltpu.SemaphoreType.DMA((6,)),
            pltpu.SemaphoreType.DMA((J, 3)),
            pltpu.SemaphoreType.DMA((J, 3)),
            pltpu.SemaphoreType.DMA((J, 3)),
            pltpu.SemaphoreType.DMA((J, 3)),
            pltpu.SemaphoreType.DMA((J,)),
            pltpu.SemaphoreType.DMA((J,)),
            pltpu.SemaphoreType.DMA((2,)),
            pltpu.SemaphoreType.DMA((2,)),
            pltpu.SemaphoreType.DMA((2,)),
            pltpu.SemaphoreType.DMA((2,)),
            pltpu.SemaphoreType.DMA((J, 3)),
        ],
        compiler_params=pltpu.CompilerParams(
            collective_id=0, has_side_effects=True, vmem_limit_bytes=48 * 1024 * 1024
        ),
        name="render",
    )(
        *(
            pltpu.with_memory_space_constraint(operand, pltpu.HBM)
            for operand in (coeffs.reshape(24, 128, N), table_z, table_y, table_take, table_x)
        )
    )
    current, picture = pl.pallas_call(
        write_out,
        out_shape=(pltpu.HBM((3, 16, 64, N), F32), pltpu.HBM((4, 16, 64), F32)),
        in_specs=[any_space, any_space],
        out_specs=(any_space, any_space),
        scratch_shapes=[pltpu.SemaphoreType.DMA((13,))],
        compiler_params=pltpu.CompilerParams(vmem_limit_bytes=4 * 1024 * 1024),
        name="write_out",
    )(*(pltpu.with_memory_space_constraint(operand, pltpu.VMEM) for operand in (current, picture)))
    return (current, picture.transpose(0, 2, 1))


def solution(mesh):
    return jax.shard_map(
        shards,
        mesh=mesh,
        in_specs=(P(None, "gy", "gz", None),),
        out_specs=(P(None, "gy", "gz", None), P(None, "gz", "gy")),
        check_vma=False,
    )
```
